32 devices in a mesh: dp: 16 (over z, x, core), ctx: 2 (over y).
Axes of the slice: x: 2, y: 2, z: 4, core: 2. Of those that a mesh axis runs over, the one named last changes fastest.
Arguments:
- layer_input: bfloat16 [16, 256, 2048], P('dp', 'ctx'), may hold values from -6 to 6
- queries: bfloat16 [16, 256, 2048], P('dp', 'ctx'), may hold values from -26.25 to 26.25
- key_states: bfloat16 [16, 256, 2048], P('dp', 'ctx'), may hold values from -10.5 to 10.5
- value_states: bfloat16 [16, 256, 2048], P('dp', 'ctx'), may hold values from -6 to 6
- out_grad: bfloat16 [16, 256, 2048], P('dp', 'ctx'), may hold values from -6 to 6
- block_kinds: int32 [16, 1], P('dp'), may hold values 0 or 1
Outputs:
- query_grad: bfloat16 [16, 256, 2048], P('dp', 'ctx')
- key_grad: bfloat16 [16, 256, 2048], P('dp', 'ctx')
- value_grad: bfloat16 [16, 256, 2048], P('dp', 'ctx')
- value_weight_gradient: float32 [2048, 2048], P('dp', 'ctx')
The draws below stay inside these ranges and needn't reach their ends.
Inputs may be any that keep to these rules, and one draw needn't show every extreme that they name: `block_kinds`: 1 marks a frame block of 256 positions, whose positions see each other; 0 marks a text block, causal inside.
All inputs are finite; a program needn't handle non-finite values.
Results may differ from the reference program's by a relative error of at most 0.012.
Values may be sent and summed in bfloat16 or wider, within the bound.
A program may use at most 64 MiB of HBM per device.

```python
import jax
import jax.numpy as jnp
from jax import lax

TOK_DEV = 128
FRAME = 256
HEADS = 16
HEAD_DIM = 128
D_IN = 2048
ATT_WIDTH = 2048
LEN = 256
BATCH = 16
NBLK = 1
N_CTX = 2


def draw_key_states(key, part):
    key = jax.random.fold_in(key, 5)
    drawn = jax.random.normal(key, (BATCH, LEN, ATT_WIDTH), jnp.float32)
    return jnp.clip(drawn, -4.0, 4.0).astype(jnp.bfloat16)


def draw_queries(key, part):
    key = jax.random.fold_in(key, 9)
    drawn = jax.random.normal(key, (BATCH, LEN, ATT_WIDTH), jnp.float32)
    return jnp.clip(drawn, -4.0, 4.0).astype(jnp.bfloat16)


def touch_ends(entries, own_key, least, high):
    longest = entries.shape.index(max(entries.shape))
    spots = []
    for shift in (0, 1):
        where = [jax.random.randint(jax.random.fold_in(own_key, axis), (), 0, length) for axis, length in enumerate(entries.shape)]
        where[longest] = (where[longest] + shift) % entries.shape[longest]
        spots.append(tuple(where))
    return entries.at[spots[0]].set(least).at[spots[1]].set(high)


def steps_of(rng, shape, pieces, low, largest):
    loudness = 1.0
    for position, blocks in pieces:
        draws = jax.random.uniform(jax.random.fold_in(jax.random.fold_in(rng, 6), position), (blocks,), jnp.float32, low / len(pieces), largest / len(pieces))
        loudness = loudness * jnp.repeat(jnp.exp(draws), shape[position] // blocks).reshape((-1,) + (1,) * (len(shape) - 1 - position))
    return loudness


def scatter_about(own_key, shape, width, limit, pieces=(), kind=jnp.bfloat16):
    loudness = steps_of(own_key, shape, pieces, -0.22, 0.18) if pieces else 1.0
    result = jax.random.normal(own_key, shape, jnp.float32) * width * loudness
    return jnp.minimum(jnp.maximum(result, -limit), limit).astype(kind)


def setup_inputs(seed: int = 0) -> dict:
    seeds = jax.random.split(jax.random.key(seed), 7)
    return {
        "layer_input": scatter_about(seeds[0], (BATCH, LEN, D_IN), 1.0, 6.0, ((0, 16), (1, 2))),
        "queries": draw_queries(jax.random.fold_in(seeds[6], 71), 0),
        "key_states": draw_key_states(jax.random.fold_in(seeds[6], 71), 0),
        "value_states": scatter_about(seeds[3], (BATCH, LEN, ATT_WIDTH), 1.0, 6.0, ((0, 16), (1, 2))),
        "out_grad": scatter_about(seeds[4], (BATCH, LEN, ATT_WIDTH), 1.0, 6.0, ((0, 16), (1, 2))),
        "block_kinds": touch_ends((jax.random.randint(seeds[5], (BATCH, NBLK), 0, 2) < 1).astype(jnp.int32), jax.random.fold_in(seeds[5], 1), 0, 1),
    }


NEG_FILL = -1.0e30


def allowed_pairs(block_kinds):
    positions = jnp.arange(LEN, dtype=jnp.int32)
    block_ids = positions // FRAME
    frame_rows = jnp.take(block_kinds, block_ids) == 1
    same_block = block_ids[None, :] == block_ids[:, None]
    return (positions[None, :] <= positions[:, None]) | (same_block & frame_rows[:, None])


def split_heads(array):
    return array.astype(jnp.float32).reshape(LEN, HEADS, HEAD_DIM).transpose(1, 0, 2)


def merge_heads(array):
    return array.transpose(1, 0, 2).reshape(LEN, HEADS * HEAD_DIM).astype(jnp.bfloat16)


def one_sequence(layer_input, queries, key_states, value_states, out_grad, block_kinds):
    score_scale = HEAD_DIM ** -0.5
    allowed = allowed_pairs(block_kinds)[None]
    q_heads = split_heads(queries)
    k_heads = split_heads(key_states)
    v_heads = split_heads(value_states)
    g_heads = split_heads(out_grad)
    attention_scores = jnp.einsum("hid,hjd->hij", q_heads, k_heads) * score_scale
    row_peak = jnp.max(jnp.where(allowed, attention_scores, NEG_FILL), axis=2, keepdims=True)
    row_total = jnp.sum(jnp.where(allowed, jnp.exp(attention_scores - row_peak), 0.0), axis=2, keepdims=True)
    log_total = row_peak + jnp.log(row_total)
    weights = jnp.where(allowed, jnp.exp(attention_scores - log_total), 0.0)
    weights_half = weights.astype(jnp.bfloat16)
    grad_probs = jnp.einsum("hid,hjd->hij", g_heads, v_heads)
    row_delta = jnp.sum(weights * grad_probs, axis=2, keepdims=True)
    grad_scores = (weights * (grad_probs - row_delta) * score_scale).astype(jnp.bfloat16)
    grad_wide = grad_scores.astype(jnp.float32)
    shard_keys = k_heads.reshape(HEADS, N_CTX, TOK_DEV, HEAD_DIM)
    key_partials = jnp.einsum("hisj,hsjd->hisd", grad_wide.reshape(HEADS, LEN, N_CTX, TOK_DEV), shard_keys)
    key_partials = lax.optimization_barrier(key_partials.astype(jnp.bfloat16))
    query_grad = jnp.sum(key_partials.astype(jnp.float32), axis=2)
    key_grad = jnp.einsum("hij,hid->hjd", grad_wide, q_heads)
    value_grad = merge_heads(jnp.einsum("hij,hid->hjd", weights_half.astype(jnp.float32), g_heads))
    weight_term = jnp.dot(layer_input.T, value_grad, preferred_element_type=jnp.float32)
    return merge_heads(query_grad), merge_heads(key_grad), value_grad, weight_term


def reference(layer_input, queries, key_states, value_states, out_grad, block_kinds):
    def advance(summed, inputs):
        query_grad, key_grad, value_grad, weight_term = one_sequence(*inputs)
        return summed + weight_term, (query_grad, key_grad, value_grad)

    start_value = jnp.zeros((D_IN, HEADS * HEAD_DIM), jnp.float32)
    weight_grad, grads = lax.scan(advance, start_value, (layer_input, queries, key_states, value_states, out_grad, block_kinds))
    return grads[0], grads[1], grads[2], weight_grad
```

```python
import functools

import jax
import jax.numpy as jnp
from jax import lax
from jax.experimental import pallas as pl
from jax.experimental.pallas import tpu as pltpu
from jax.sharding import PartitionSpec as P

FRAME = 256
HEAD_DIM = 128
D_IN = 2048


NEG_FILL = -1e30


def tile_scores(query_tile, key_block):
    product = jnp.einsum("ihd,jhd->hij", query_tile, key_block, preferred_element_type=jnp.float32)
    return product * HEAD_DIM ** (-0.5)


def tile_mask(row_start, key_start, key_count, block_kinds):
    query_pos = row_start + lax.iota(jnp.int32, FRAME)
    key_positions = key_start + lax.iota(jnp.int32, key_count)
    frame_flag = lax.dynamic_index_in_dim(block_kinds, row_start // FRAME, keepdims=False) == 1
    same_block = (key_positions // FRAME)[None, :] == (query_pos // FRAME)[:, None]
    return ((key_positions[None, :] <= query_pos[:, None]) | same_block & frame_flag)[None]


def rows_of(complete_rows, tile_index):
    return lax.dynamic_slice_in_dim(complete_rows, tile_index * FRAME, FRAME, 0)


def cols_of(stat_rows, tile_index):
    return lax.dynamic_slice_in_dim(stat_rows, tile_index * FRAME, FRAME, 1)


def put_cols(stat_rows, new_part, tile_index):
    return lax.dynamic_update_slice_in_dim(stat_rows, new_part, tile_index * FRAME, 1)


def head_split(stat_rows, work_items):
    pieces_out = []
    for work_item in work_items:
        pieces_out.append(stat_rows)
    return pieces_out


def sweep_peak(work_item, block_kinds):
    query_h, grad_h, key_block, value_block, key_start = work_item

    def advance(tile_index, peak_now):
        attention_scores = tile_scores(rows_of(query_h, tile_index), key_block)
        allowed = tile_mask(tile_index * FRAME, key_start, key_block.shape[0], block_kinds)
        return put_cols(
            peak_now, jnp.max(jnp.where(allowed, attention_scores, NEG_FILL), axis=2), tile_index
        )

    start_value = jnp.full((key_block.shape[1], query_h.shape[0]), NEG_FILL, jnp.float32)
    return lax.fori_loop(key_start // FRAME, query_h.shape[0] // FRAME, advance, start_value)


def sweep_total(work_item, block_kinds, peak_rows):
    query_h, grad_h, key_block, value_block, key_start = work_item

    def advance(tile_index, total_now):
        attention_scores = tile_scores(rows_of(query_h, tile_index), key_block)
        allowed = tile_mask(tile_index * FRAME, key_start, key_block.shape[0], block_kinds)
        shifted = jnp.exp(attention_scores - cols_of(peak_rows, tile_index)[:, :, None])
        return put_cols(total_now, jnp.sum(jnp.where(allowed, shifted, 0.0), axis=2), tile_index)

    start_value = jnp.zeros((key_block.shape[1], query_h.shape[0]), jnp.float32)
    return lax.fori_loop(key_start // FRAME, query_h.shape[0] // FRAME, advance, start_value)


def sweep_delta(work_item, block_kinds, log_rows):
    query_h, grad_h, key_block, value_block, key_start = work_item

    def advance(tile_index, delta_now):
        attention_scores = tile_scores(rows_of(query_h, tile_index), key_block)
        allowed = tile_mask(tile_index * FRAME, key_start, key_block.shape[0], block_kinds)
        weights = jnp.where(
            allowed, jnp.exp(attention_scores - cols_of(log_rows, tile_index)[:, :, None]), 0.0
        )
        grad_probs = jnp.einsum(
            "ihd,jhd->hij",
            rows_of(grad_h, tile_index),
            value_block,
            preferred_element_type=jnp.float32,
        )
        return put_cols(delta_now, jnp.sum(weights * grad_probs, axis=2), tile_index)

    start_value = jnp.zeros((key_block.shape[1], query_h.shape[0]), jnp.float32)
    return lax.fori_loop(key_start // FRAME, query_h.shape[0] // FRAME, advance, start_value)


def sweep_grads(work_item, block_kinds, log_rows, delta_rows):
    query_h, grad_h, key_block, value_block, key_start = work_item
    score_scale = HEAD_DIM ** (-0.5)

    def advance(tile_index, carry):
        key_acc, value_acc, dq_term = carry
        query_tile = rows_of(query_h, tile_index)
        gradient_piece = rows_of(grad_h, tile_index)
        attention_scores = tile_scores(query_tile, key_block)
        allowed = tile_mask(tile_index * FRAME, key_start, key_block.shape[0], block_kinds)
        weights = jnp.where(
            allowed, jnp.exp(attention_scores - cols_of(log_rows, tile_index)[:, :, None]), 0.0
        )
        grad_probs = jnp.einsum(
            "ihd,jhd->hij", gradient_piece, value_block, preferred_element_type=jnp.float32
        )
        grad_scores = (
            weights * (grad_probs - cols_of(delta_rows, tile_index)[:, :, None]) * score_scale
        ).astype(jnp.bfloat16)
        weights_half = weights.astype(jnp.bfloat16)
        value_acc = value_acc + jnp.einsum(
            "hij,ihd->jhd", weights_half, gradient_piece, preferred_element_type=jnp.float32
        )
        key_acc = key_acc + jnp.einsum(
            "hij,ihd->jhd", grad_scores, query_tile, preferred_element_type=jnp.float32
        )
        query_rows_part = jnp.einsum(
            "hij,jhd->ihd", grad_scores, key_block, preferred_element_type=jnp.float32
        )
        dq_term = lax.dynamic_update_slice_in_dim(dq_term, query_rows_part, tile_index * FRAME, 0)
        return (key_acc, value_acc, dq_term)

    start_value = (
        jnp.zeros(key_block.shape, jnp.float32),
        jnp.zeros(key_block.shape, jnp.float32),
        jnp.zeros(query_h.shape, jnp.float32),
    )
    return lax.fori_loop(key_start // FRAME, query_h.shape[0] // FRAME, advance, start_value)


def body(layer_input, queries, key_states, value_states, out_grad, block_kinds):
    shard_rows = queries.shape[1]
    row_width = queries.shape[2]
    head_count = row_width // HEAD_DIM
    ctx_size = lax.axis_size("ctx")
    dp_size = lax.axis_size("dp")
    my_index = lax.axis_index("ctx")
    kinds_row = block_kinds[0]
    query_all, grad_all = (
        lax.all_gather(queries[0], "ctx", axis=0, tiled=True),
        lax.all_gather(out_grad[0], "ctx", axis=0, tiled=True),
    )
    total_rows = query_all.shape[0]
    query_all = query_all.reshape(total_rows, head_count, HEAD_DIM)
    grad_all = grad_all.reshape(total_rows, head_count, HEAD_DIM)
    own_keys = key_states[0].reshape(shard_rows, head_count, HEAD_DIM)
    own_values = value_states[0].reshape(shard_rows, head_count, HEAD_DIM)
    own_start = my_index * shard_rows
    work_items = [(query_all, grad_all, own_keys, own_values, own_start)]
    row_peaks = jnp.concatenate(
        [sweep_peak(work_item, kinds_row) for work_item in work_items], axis=0
    )
    row_peaks = lax.pmax(row_peaks.astype(jnp.bfloat16), "ctx").astype(row_peaks.dtype)
    peak_parts = head_split(row_peaks, work_items)
    totals = jnp.concatenate(
        [
            sweep_total(work_item, kinds_row, peak_part)
            for work_item, peak_part in zip(work_items, peak_parts)
        ],
        axis=0,
    )
    totals = lax.psum(totals, "ctx")
    log_total = row_peaks + jnp.log(totals)
    log_parts = head_split(log_total, work_items)
    deltas = jnp.concatenate(
        [
            sweep_delta(work_item, kinds_row, log_part)
            for work_item, log_part in zip(work_items, log_parts)
        ],
        axis=0,
    )
    deltas = lax.psum(deltas, "ctx")
    delta_parts = head_split(deltas, work_items)
    results = [
        sweep_grads(work_item, kinds_row, log_part, delta_part)
        for work_item, log_part, delta_part in zip(work_items, log_parts, delta_parts)
    ]
    dq_term = jnp.concatenate([entry_set[2] for entry_set in results], axis=1).reshape(
        total_rows, row_width
    )
    query_grad = lax.psum_scatter(
        dq_term.astype(jnp.bfloat16), "ctx", scatter_dimension=0, tiled=True
    )
    key_grad = results[0][0].astype(jnp.bfloat16)
    value_grad = results[0][1].astype(jnp.bfloat16)
    key_grad = key_grad.reshape(shard_rows, row_width)
    value_grad = value_grad.reshape(shard_rows, row_width)
    rows_each = D_IN // dp_size
    cols_each = row_width // ctx_size
    divided_input = layer_input[0].reshape(shard_rows, dp_size, rows_each)
    divided_gradient = value_grad.reshape(shard_rows, ctx_size, cols_each)
    weight_term = jnp.einsum(
        "zkg,zbi->kbgi", divided_input, divided_gradient, preferred_element_type=jnp.float32
    )
    weight_term = weight_term.reshape(dp_size * ctx_size * rows_each, cols_each)
    weight_grad = lax.psum_scatter(weight_term, ("dp", "ctx"), scatter_dimension=0, tiled=True)
    return (query_grad[None], key_grad[None], value_grad[None], weight_grad)


HEADS_PER_CHUNK = 2
CHUNK = HEADS_PER_CHUNK * HEAD_DIM
MESH = pl.DeviceIdType.MESH
F32 = jnp.float32
BF16 = jnp.bfloat16
SCALE = HEAD_DIM ** (-0.5)
PLANE = [(dx, dc, dy) for dx in (0, 1) for dc in (0, 1) for dy in (0, 1)]


def dot_last(a, b):
    return lax.dot_general(a, b, (((1,), (1,)), ((), ())), preferred_element_type=F32)


def dot_first(a, b):
    return lax.dot_general(a, b, (((0,), (0,)), ((), ())), preferred_element_type=F32)


def dot_plain(a, b):
    return lax.dot_general(a, b, (((1,), (0,)), ((), ())), preferred_element_type=F32)


def fused_kernel(
    sizes,
    kinds,
    x_in,
    q_in,
    k_in,
    v_in,
    g_in,
    dq_out,
    dk_out,
    dv_out,
    w_out,
    qkvg,
    dq_s,
    dk_s,
    vall,
    lall,
    lt,
    w_send,
    w_recv,
    w_own,
    in_send,
    in_recv,
    in_local,
    l_send,
    l_recv,
    l_local,
    v_send,
    v_recv,
    r_send,
    r_recv,
    o_local,
    z_send,
    z_recv,
    w_local,
):
    rows, half, nz, chunks = sizes
    seq = 2 * rows
    each = HEAD_DIM
    dp = lax.axis_index("dp")
    y = lax.axis_index("ctx")
    c = lax.rem(dp, 2)
    x = lax.rem(dp // 2, 2)
    z = dp // 4
    yp = 1 - y

    def plane_id(dx, dc, dy):
        xx = lax.rem(x + dx, 2)
        cc = lax.rem(c + dc, 2)
        yy = lax.rem(y + dy, 2)
        return ((z * 2 + xx) * 2 + cc, yy), xx, cc

    def z_id(dz):
        return (lax.rem(z + dz, nz) * 4 + x * 2 + c, y)

    barrier = pltpu.get_barrier_semaphore()
    for dx, dc, dy in PLANE[1:]:
        pl.semaphore_signal(barrier, inc=1, device_id=plane_id(dx, dc, dy)[0], device_id_type=MESH)
    for dz in range(1, nz):
        pl.semaphore_signal(barrier, inc=1, device_id=z_id(dz), device_id_type=MESH)

    def aligned(value):
        return pl.multiple_of(value, 128)

    my_rows = pl.ds(aligned(y * rows), rows)
    peer_rows = pl.ds(aligned(yp * rows), rows)

    def remote(src, dst, send_sem, recv_sem, device):
        return pltpu.make_async_remote_copy(
            src_ref=src,
            dst_ref=dst,
            send_sem=send_sem,
            recv_sem=recv_sem,
            device_id=device,
            device_id_type=MESH,
        )

    sources = (q_in, k_in, v_in, g_in)
    local_in = []
    for n in range(chunks):
        cols = pl.ds(n * CHUNK, CHUNK)
        mine = pl.ds(aligned(y * half + n * CHUNK), CHUNK)
        local_in.append(
            [
                pltpu.make_async_copy(
                    src.at[:, mine], qkvg.at[t, my_rows, cols], in_local.at[n, t]
                )
                for t, src in enumerate(sources)
            ]
        )
    for copies in local_in:
        for copy in copies:
            copy.start()
    l_own = []
    for dz in range(nz):
        col = pl.ds(aligned((lax.rem(z + dz, nz) * 4 + x * 2 + c) * each), each)
        l_own.append(
            pltpu.make_async_copy(
                x_in.at[:, col], lall.at[my_rows, pl.ds(dz * each, each)], l_local.at[dz]
            )
        )
        l_own[-1].start()

    pl.semaphore_wait(barrier, 7 + nz - 1)

    peer_id = plane_id(0, 0, 1)[0]
    sends_in = []
    for n in range(chunks):
        cols = pl.ds(n * CHUNK, CHUNK)
        theirs = pl.ds(aligned(yp * half + n * CHUNK), CHUNK)
        sends_in.append(
            [
                remote(
                    src.at[:, theirs],
                    qkvg.at[t, my_rows, cols],
                    in_send.at[n, t],
                    in_recv.at[n, t],
                    peer_id,
                )
                for t, src in enumerate(sources)
            ]
        )
    sends_l = []
    for p, (dx, dc, dy) in enumerate(PLANE):
        if p == 0:
            continue
        device, xx, cc = plane_id(dx, dc, dy)
        slot = dx * 2 + dc
        dst_rows = pl.ds(aligned(slot * seq + y * rows), rows)
        for dz in range(nz):
            col = pl.ds(aligned((lax.rem(z + dz, nz) * 4 + xx * 2 + cc) * each), each)
            sends_l.append(
                remote(
                    x_in.at[:, col],
                    lall.at[dst_rows, pl.ds(dz * each, each)],
                    l_send.at[p - 1, dz],
                    l_recv.at[p - 1, dz],
                    device,
                )
            )
    for n in range(chunks):
        for copy in sends_in[n]:
            copy.start()
        if n == 0:
            for copy in sends_l:
                copy.start()

    key_pos = lax.broadcasted_iota(jnp.int32, (seq, seq), 0)
    query_pos = lax.broadcasted_iota(jnp.int32, (seq, seq), 1)
    allowed = key_pos <= query_pos + kinds[0, 0] * seq

    def head(h):
        hc = pl.ds(h * HEAD_DIM, HEAD_DIM)
        q = qkvg[0, :, hc]
        k = qkvg[1, :, hc]
        v = qkvg[2, :, hc]
        g = qkvg[3, :, hc]
        scores = jnp.where(allowed, dot_last(k, q) * SCALE, NEG_FILL)
        peak = jnp.max(scores, axis=0, keepdims=True)
        p = jnp.exp(scores - peak)
        weights = p * (1.0 / jnp.sum(p, axis=0, keepdims=True))
        weights_half = weights.astype(BF16)
        vall[pl.ds(0, seq), hc] = dot_plain(weights_half, g).astype(BF16)
        grad_probs = dot_last(v, g)
        delta = jnp.sum(weights * grad_probs, axis=0, keepdims=True)
        grad_scores = (weights * (grad_probs - delta) * SCALE).astype(BF16)
        dk_s[:, hc] = dot_plain(grad_scores, q).astype(BF16)
        parts = [
            dot_first(grad_scores[s * rows : (s + 1) * rows], k[s * rows : (s + 1) * rows])
            .astype(BF16)
            .astype(F32)
            for s in range(2)
        ]
        dq_s[:, hc] = (parts[0] + parts[1]).astype(BF16)

    v_copies, r_copies, z_copies, o_copies = [], [], [], []

    def attention(n):
        for t in range(4):
            local_in[n][t].wait()
            sends_in[n][t].wait_recv()
        for j in range(HEADS_PER_CHUNK):
            head(n * HEADS_PER_CHUNK + j)
        cols = pl.ds(n * CHUNK, CHUNK)
        group = []
        for slot in (2, 3, 1):
            group.append(
                remote(
                    vall.at[pl.ds(0, seq), cols],
                    vall.at[pl.ds(slot * seq, seq), cols],
                    v_send.at[n, slot - 1],
                    v_recv.at[n, slot - 1],
                    plane_id(slot // 2, slot % 2, 0)[0],
                )
            )
            group[-1].start()
        v_copies.append(group)
        out_cols = pl.ds(aligned(y * half + n * CHUNK), CHUNK)
        results = ((vall, dv_out), (dk_s, dk_out), (dq_s, dq_out))
        group = []
        for t, (src, dst) in enumerate(results):
            group.append(
                remote(
                    src.at[peer_rows, cols],
                    dst.at[:, out_cols],
                    r_send.at[n, t],
                    r_recv.at[n, t],
                    peer_id,
                )
            )
            group[-1].start()
        r_copies.append(group)
        group = []
        for t, (src, dst) in enumerate(results):
            group.append(
                pltpu.make_async_copy(
                    src.at[my_rows, cols], dst.at[:, out_cols], o_local.at[n, t]
                )
            )
            group[-1].start()
        o_copies.append(group)

    def weight(n):
        for copy in v_copies[n]:
            copy.wait_recv()
        cols = pl.ds(n * CHUNK, CHUNK)
        term = dot_plain(lt[...], vall[:, cols])
        w_own[:, cols] = term[:each]
        group = []
        for dz in range(1, nz):
            w_send[dz - 1, :, cols] = term[dz * each : (dz + 1) * each].astype(BF16)
            group.append(
                remote(
                    w_send.at[dz - 1, :, cols],
                    w_recv.at[dz - 1, :, cols],
                    z_send.at[n, dz - 1],
                    z_recv.at[n, dz - 1],
                    z_id(dz),
                )
            )
            group[-1].start()
        z_copies.append(group)

    attention(0)
    for n in range(1, chunks):
        attention(n)
        if n == 1:
            for copy in l_own:
                copy.wait()
            for copy in sends_l:
                copy.wait_recv()
            for s in range(4):
                lt[:, pl.ds(s * seq, seq)] = lall[pl.ds(s * seq, seq), :].T
        weight(n - 1)
    weight(chunks - 1)

    w_copies = []
    for n in range(chunks):
        cols = pl.ds(n * CHUNK, CHUNK)
        total = w_own[:, cols]
        for dz in range(1, nz):
            z_copies[n][dz - 1].wait_recv()
            total = total + w_recv[dz - 1, :, cols].astype(F32)
        w_own[:, cols] = total
        w_copies.append(
            pltpu.make_async_copy(w_own.at[:, cols], w_out.at[:, cols], w_local.at[n])
        )
        w_copies[-1].start()

    for copies in sends_in + v_copies + z_copies + [sends_l]:
        for copy in copies:
            copy.wait_send()
    for copies in r_copies + o_copies + [w_copies]:
        for copy in copies:
            copy.wait()


def fused_body(layer_input, queries, key_states, value_states, out_grad, block_kinds):
    rows, width = queries.shape[1:]
    half = width // 2
    nz = lax.axis_size("dp") // 4
    chunks = half // CHUNK
    seq = 2 * rows
    depth = 4 * seq
    each = HEAD_DIM
    dma = pltpu.SemaphoreType.DMA
    half_out = jax.ShapeDtypeStruct((rows, width), BF16)
    outs = pl.pallas_call(
        functools.partial(fused_kernel, (rows, half, nz, chunks)),
        out_shape=(half_out, half_out, half_out, jax.ShapeDtypeStruct((each, half), F32)),
        in_specs=[pl.BlockSpec(memory_space=pltpu.SMEM)]
        + [pl.BlockSpec(memory_space=pl.ANY)] * 5,
        out_specs=[pl.BlockSpec(memory_space=pl.ANY)] * 4,
        scratch_shapes=[
            pltpu.VMEM((4, seq, half), BF16),
            pltpu.VMEM((seq, half), BF16),
            pltpu.VMEM((seq, half), BF16),
            pltpu.VMEM((depth, half), BF16),
            pltpu.VMEM((depth, nz * each), BF16),
            pltpu.VMEM((nz * each, depth), BF16),
            pltpu.VMEM((nz - 1, each, half), BF16),
            pltpu.VMEM((nz - 1, each, half), BF16),
            pltpu.VMEM((each, half), F32),
            dma((chunks, 4)),
            dma((chunks, 4)),
            dma((chunks, 4)),
            dma((7, nz)),
            dma((7, nz)),
            dma((nz,)),
            dma((chunks, 3)),
            dma((chunks, 3)),
            dma((chunks, 3)),
            dma((chunks, 3)),
            dma((chunks, 3)),
            dma((chunks, nz - 1)),
            dma((chunks, nz - 1)),
            dma((chunks,)),
        ],
        compiler_params=pltpu.CompilerParams(
            collective_id=0, has_side_effects=True, vmem_limit_bytes=48 * 1024 * 1024
        ),
        cost_estimate=pl.CostEstimate(
            flops=2 * (5 * seq * seq * half + depth * nz * each * half),
            bytes_accessed=8 * rows * width * 2 + each * half * 4,
            transcendentals=seq * seq * half // HEAD_DIM,
        ),
    )(block_kinds, layer_input[0], queries[0], key_states[0], value_states[0], out_grad[0])
    return (outs[0][None], outs[1][None], outs[2][None], outs[3])


def pick_body(mesh):
    ctx_size, dp_size = mesh.shape["ctx"], mesh.shape["dp"]

    def chosen(layer_input, queries, *others):
        fits = (
            ctx_size == 2
            and dp_size % 4 == 0
            and dp_size > 4
            and dp_size * HEAD_DIM == D_IN
            and queries.shape[0] == 1
            and 2 * queries.shape[1] == FRAME
            and queries.shape[2] % (2 * CHUNK) == 0
        )
        return (fused_body if fits else body)(layer_input, queries, *others)

    return chosen


def solution(mesh):
    return jax.shard_map(
        pick_body(mesh),
        mesh=mesh,
        in_specs=(
            P("dp", "ctx", None),
            P("dp", "ctx", None),
            P("dp", "ctx", None),
            P("dp", "ctx", None),
            P("dp", "ctx", None),
            P("dp", None),
        ),
        out_specs=(
            P("dp", "ctx", None),
            P("dp", "ctx", None),
            P("dp", "ctx", None),
            P("dp", "ctx"),
        ),
        check_vma=False,
    )
```

```python
import functools

import jax
import jax.numpy as jnp
from jax import lax
from jax.experimental import pallas as pl
from jax.experimental.pallas import tpu as pltpu
from jax.sharding import PartitionSpec as P

FRAME = 256
HEAD_DIM = 128
D_IN = 2048


NEG_FILL = -1e30


def tile_scores(query_tile, key_block):
    product = jnp.einsum("ihd,jhd->hij", query_tile, key_block, preferred_element_type=jnp.float32)
    return product * HEAD_DIM ** (-0.5)


def tile_mask(row_start, key_start, key_count, block_kinds):
    query_pos = row_start + lax.iota(jnp.int32, FRAME)
    key_positions = key_start + lax.iota(jnp.int32, key_count)
    frame_flag = lax.dynamic_index_in_dim(block_kinds, row_start // FRAME, keepdims=False) == 1
    same_block = (key_positions // FRAME)[None, :] == (query_pos // FRAME)[:, None]
    return ((key_positions[None, :] <= query_pos[:, None]) | same_block & frame_flag)[None]


def rows_of(complete_rows, tile_index):
    return lax.dynamic_slice_in_dim(complete_rows, tile_index * FRAME, FRAME, 0)


def cols_of(stat_rows, tile_index):
    return lax.dynamic_slice_in_dim(stat_rows, tile_index * FRAME, FRAME, 1)


def put_cols(stat_rows, new_part, tile_index):
    return lax.dynamic_update_slice_in_dim(stat_rows, new_part, tile_index * FRAME, 1)


def head_split(stat_rows, work_items):
    pieces_out = []
    for work_item in work_items:
        pieces_out.append(stat_rows)
    return pieces_out


def sweep_peak(work_item, block_kinds):
    query_h, grad_h, key_block, value_block, key_start = work_item

    def advance(tile_index, peak_now):
        attention_scores = tile_scores(rows_of(query_h, tile_index), key_block)
        allowed = tile_mask(tile_index * FRAME, key_start, key_block.shape[0], block_kinds)
        return put_cols(
            peak_now, jnp.max(jnp.where(allowed, attention_scores, NEG_FILL), axis=2), tile_index
        )

    start_value = jnp.full((key_block.shape[1], query_h.shape[0]), NEG_FILL, jnp.float32)
    return lax.fori_loop(key_start // FRAME, query_h.shape[0] // FRAME, advance, start_value)


def sweep_total(work_item, block_kinds, peak_rows):
    query_h, grad_h, key_block, value_block, key_start = work_item

    def advance(tile_index, total_now):
        attention_scores = tile_scores(rows_of(query_h, tile_index), key_block)
        allowed = tile_mask(tile_index * FRAME, key_start, key_block.shape[0], block_kinds)
        shifted = jnp.exp(attention_scores - cols_of(peak_rows, tile_index)[:, :, None])
        return put_cols(total_now, jnp.sum(jnp.where(allowed, shifted, 0.0), axis=2), tile_index)

    start_value = jnp.zeros((key_block.shape[1], query_h.shape[0]), jnp.float32)
    return lax.fori_loop(key_start // FRAME, query_h.shape[0] // FRAME, advance, start_value)


def sweep_delta(work_item, block_kinds, log_rows):
    query_h, grad_h, key_block, value_block, key_start = work_item

    def advance(tile_index, delta_now):
        attention_scores = tile_scores(rows_of(query_h, tile_index), key_block)
        allowed = tile_mask(tile_index * FRAME, key_start, key_block.shape[0], block_kinds)
        weights = jnp.where(
            allowed, jnp.exp(attention_scores - cols_of(log_rows, tile_index)[:, :, None]), 0.0
        )
        grad_probs = jnp.einsum(
            "ihd,jhd->hij",
            rows_of(grad_h, tile_index),
            value_block,
            preferred_element_type=jnp.float32,
        )
        return put_cols(delta_now, jnp.sum(weights * grad_probs, axis=2), tile_index)

    start_value = jnp.zeros((key_block.shape[1], query_h.shape[0]), jnp.float32)
    return lax.fori_loop(key_start // FRAME, query_h.shape[0] // FRAME, advance, start_value)


def sweep_grads(work_item, block_kinds, log_rows, delta_rows):
    query_h, grad_h, key_block, value_block, key_start = work_item
    score_scale = HEAD_DIM ** (-0.5)

    def advance(tile_index, carry):
        key_acc, value_acc, dq_term = carry
        query_tile = rows_of(query_h, tile_index)
        gradient_piece = rows_of(grad_h, tile_index)
        attention_scores = tile_scores(query_tile, key_block)
        allowed = tile_mask(tile_index * FRAME, key_start, key_block.shape[0], block_kinds)
        weights = jnp.where(
            allowed, jnp.exp(attention_scores - cols_of(log_rows, tile_index)[:, :, None]), 0.0
        )
        grad_probs = jnp.einsum(
            "ihd,jhd->hij", gradient_piece, value_block, preferred_element_type=jnp.float32
        )
        grad_scores = (
            weights * (grad_probs - cols_of(delta_rows, tile_index)[:, :, None]) * score_scale
        ).astype(jnp.bfloat16)
        weights_half = weights.astype(jnp.bfloat16)
        value_acc = value_acc + jnp.einsum(
            "hij,ihd->jhd", weights_half, gradient_piece, preferred_element_type=jnp.float32
        )
        key_acc = key_acc + jnp.einsum(
            "hij,ihd->jhd", grad_scores, query_tile, preferred_element_type=jnp.float32
        )
        query_rows_part = jnp.einsum(
            "hij,jhd->ihd", grad_scores, key_block, preferred_element_type=jnp.float32
        )
        dq_term = lax.dynamic_update_slice_in_dim(dq_term, query_rows_part, tile_index * FRAME, 0)
        return (key_acc, value_acc, dq_term)

    start_value = (
        jnp.zeros(key_block.shape, jnp.float32),
        jnp.zeros(key_block.shape, jnp.float32),
        jnp.zeros(query_h.shape, jnp.float32),
    )
    return lax.fori_loop(key_start // FRAME, query_h.shape[0] // FRAME, advance, start_value)


def body(layer_input, queries, key_states, value_states, out_grad, block_kinds):
    shard_rows = queries.shape[1]
    row_width = queries.shape[2]
    head_count = row_width // HEAD_DIM
    ctx_size = lax.axis_size("ctx")
    dp_size = lax.axis_size("dp")
    my_index = lax.axis_index("ctx")
    kinds_row = block_kinds[0]
    query_all, grad_all = (
        lax.all_gather(queries[0], "ctx", axis=0, tiled=True),
        lax.all_gather(out_grad[0], "ctx", axis=0, tiled=True),
    )
    total_rows = query_all.shape[0]
    query_all = query_all.reshape(total_rows, head_count, HEAD_DIM)
    grad_all = grad_all.reshape(total_rows, head_count, HEAD_DIM)
    own_keys = key_states[0].reshape(shard_rows, head_count, HEAD_DIM)
    own_values = value_states[0].reshape(shard_rows, head_count, HEAD_DIM)
    own_start = my_index * shard_rows
    work_items = [(query_all, grad_all, own_keys, own_values, own_start)]
    row_peaks = jnp.concatenate(
        [sweep_peak(work_item, kinds_row) for work_item in work_items], axis=0
    )
    row_peaks = lax.pmax(row_peaks.astype(jnp.bfloat16), "ctx").astype(row_peaks.dtype)
    peak_parts = head_split(row_peaks, work_items)
    totals = jnp.concatenate(
        [
            sweep_total(work_item, kinds_row, peak_part)
            for work_item, peak_part in zip(work_items, peak_parts)
        ],
        axis=0,
    )
    totals = lax.psum(totals, "ctx")
    log_total = row_peaks + jnp.log(totals)
    log_parts = head_split(log_total, work_items)
    deltas = jnp.concatenate(
        [
            sweep_delta(work_item, kinds_row, log_part)
            for work_item, log_part in zip(work_items, log_parts)
        ],
        axis=0,
    )
    deltas = lax.psum(deltas, "ctx")
    delta_parts = head_split(deltas, work_items)
    results = [
        sweep_grads(work_item, kinds_row, log_part, delta_part)
        for work_item, log_part, delta_part in zip(work_items, log_parts, delta_parts)
    ]
    dq_term = jnp.concatenate([entry_set[2] for entry_set in results], axis=1).reshape(
        total_rows, row_width
    )
    query_grad = lax.psum_scatter(
        dq_term.astype(jnp.bfloat16), "ctx", scatter_dimension=0, tiled=True
    )
    key_grad = results[0][0].astype(jnp.bfloat16)
    value_grad = results[0][1].astype(jnp.bfloat16)
    key_grad = key_grad.reshape(shard_rows, row_width)
    value_grad = value_grad.reshape(shard_rows, row_width)
    rows_each = D_IN // dp_size
    cols_each = row_width // ctx_size
    divided_input = layer_input[0].reshape(shard_rows, dp_size, rows_each)
    divided_gradient = value_grad.reshape(shard_rows, ctx_size, cols_each)
    weight_term = jnp.einsum(
        "zkg,zbi->kbgi", divided_input, divided_gradient, preferred_element_type=jnp.float32
    )
    weight_term = weight_term.reshape(dp_size * ctx_size * rows_each, cols_each)
    weight_grad = lax.psum_scatter(weight_term, ("dp", "ctx"), scatter_dimension=0, tiled=True)
    return (query_grad[None], key_grad[None], value_grad[None], weight_grad)


HEADS_PER_CHUNK = 2
CHUNK = HEADS_PER_CHUNK * HEAD_DIM
VMEM_LIMIT = 63 * 1024 * 1024
MESH = pl.DeviceIdType.MESH
F32 = jnp.float32
BF16 = jnp.bfloat16
SCALE = HEAD_DIM ** (-0.5)
PLANE = [(dx, dc, dy) for dx in (0, 1) for dc in (0, 1) for dy in (0, 1)]


def dot_last(a, b):
    return lax.dot_general(a, b, (((1,), (1,)), ((), ())), preferred_element_type=F32)


def dot_first(a, b):
    return lax.dot_general(a, b, (((0,), (0,)), ((), ())), preferred_element_type=F32)


def dot_plain(a, b):
    return lax.dot_general(a, b, (((1,), (0,)), ((), ())), preferred_element_type=F32)


def fused_kernel(
    sizes,
    kinds,
    x_in,
    q_in,
    k_in,
    v_in,
    g_in,
    dq_out,
    dk_out,
    dv_out,
    w_out,
    qkvg,
    dq_s,
    dk_s,
    vall,
    lall,
    lt,
    w_send,
    w_recv,
    w_own,
    in_send,
    in_recv,
    in_local,
    l_send,
    l_recv,
    l_local,
    v_send,
    v_recv,
    r_send,
    r_recv,
    o_local,
    z_send,
    z_recv,
    w_local,
):
    rows, half, nz, chunks = sizes
    seq = 2 * rows
    each = HEAD_DIM
    dp = lax.axis_index("dp")
    y = lax.axis_index("ctx")
    c = lax.rem(dp, 2)
    x = lax.rem(dp // 2, 2)
    z = dp // 4
    yp = 1 - y

    def plane_id(dx, dc, dy):
        xx = lax.rem(x + dx, 2)
        cc = lax.rem(c + dc, 2)
        yy = lax.rem(y + dy, 2)
        return ((z * 2 + xx) * 2 + cc, yy), xx, cc

    def z_id(dz):
        return (lax.rem(z + dz, nz) * 4 + x * 2 + c, y)

    barrier = pltpu.get_barrier_semaphore()
    for dx, dc, dy in PLANE[1:]:
        pl.semaphore_signal(barrier, inc=1, device_id=plane_id(dx, dc, dy)[0], device_id_type=MESH)
    for dz in range(1, nz):
        pl.semaphore_signal(barrier, inc=1, device_id=z_id(dz), device_id_type=MESH)

    def aligned(value):
        return pl.multiple_of(value, 128)

    my_rows = pl.ds(aligned(y * rows), rows)
    peer_rows = pl.ds(aligned(yp * rows), rows)

    def remote(src, dst, send_sem, recv_sem, device):
        return pltpu.make_async_remote_copy(
            src_ref=src,
            dst_ref=dst,
            send_sem=send_sem,
            recv_sem=recv_sem,
            device_id=device,
            device_id_type=MESH,
        )

    sources = (q_in, k_in, v_in, g_in)
    local_in = []
    for n in range(chunks):
        cols = pl.ds(n * CHUNK, CHUNK)
        mine = pl.ds(aligned(y * half + n * CHUNK), CHUNK)
        local_in.append(
            [
                pltpu.make_async_copy(
                    src.at[:, mine], qkvg.at[t, my_rows, cols], in_local.at[n, t]
                )
                for t, src in enumerate(sources)
            ]
        )
    for copies in local_in:
        for copy in copies:
            copy.start()
    l_own = []
    for dz in range(nz):
        col = pl.ds(aligned((lax.rem(z + dz, nz) * 4 + x * 2 + c) * each), each)
        l_own.append(
            pltpu.make_async_copy(
                x_in.at[:, col], lall.at[my_rows, pl.ds(dz * each, each)], l_local.at[dz]
            )
        )
        l_own[-1].start()

    pl.semaphore_wait(barrier, 7 + nz - 1)

    peer_id = plane_id(0, 0, 1)[0]
    sends_in = []
    for n in range(chunks):
        cols = pl.ds(n * CHUNK, CHUNK)
        theirs = pl.ds(aligned(yp * half + n * CHUNK), CHUNK)
        sends_in.append(
            [
                remote(
                    src.at[:, theirs],
                    qkvg.at[t, my_rows, cols],
                    in_send.at[n, t],
                    in_recv.at[n, t],
                    peer_id,
                )
                for t, src in enumerate(sources)
            ]
        )
    sends_l = []
    for p, (dx, dc, dy) in enumerate(PLANE):
        if p == 0:
            continue
        device, xx, cc = plane_id(dx, dc, dy)
        slot = dx * 2 + dc
        dst_rows = pl.ds(aligned(slot * seq + y * rows), rows)
        for dz in range(nz):
            col = pl.ds(aligned((lax.rem(z + dz, nz) * 4 + xx * 2 + cc) * each), each)
            sends_l.append(
                remote(
                    x_in.at[:, col],
                    lall.at[dst_rows, pl.ds(dz * each, each)],
                    l_send.at[p - 1, dz],
                    l_recv.at[p - 1, dz],
                    device,
                )
            )
    for n in range(chunks):
        for copy in sends_in[n]:
            copy.start()
        if n == 0:
            for copy in sends_l:
                copy.start()

    key_pos = lax.broadcasted_iota(jnp.int32, (seq, seq), 0)
    query_pos = lax.broadcasted_iota(jnp.int32, (seq, seq), 1)
    allowed = key_pos <= query_pos + kinds[0, 0] * seq

    def head(h):
        hc = pl.ds(h * HEAD_DIM, HEAD_DIM)
        q = qkvg[0, :, hc]
        k = qkvg[1, :, hc]
        v = qkvg[2, :, hc]
        g = qkvg[3, :, hc]
        scores = jnp.where(allowed, dot_last(k, q) * SCALE, NEG_FILL)
        peak = jnp.max(scores, axis=0, keepdims=True)
        p = jnp.exp(scores - peak)
        weights = p * (1.0 / jnp.sum(p, axis=0, keepdims=True))
        weights_half = weights.astype(BF16)
        vall[pl.ds(0, seq), hc] = dot_plain(weights_half, g).astype(BF16)
        grad_probs = dot_last(v, g)
        delta = jnp.sum(weights * grad_probs, axis=0, keepdims=True)
        grad_scores = (weights * (grad_probs - delta) * SCALE).astype(BF16)
        dk_s[:, hc] = dot_plain(grad_scores, q).astype(BF16)
        parts = [
            dot_first(grad_scores[s * rows : (s + 1) * rows], k[s * rows : (s + 1) * rows])
            .astype(BF16)
            .astype(F32)
            for s in range(2)
        ]
        dq_s[:, hc] = (parts[0] + parts[1]).astype(BF16)

    v_copies, r_copies, z_copies, o_copies = [], [], [], []

    def attention(n):
        for t in range(4):
            local_in[n][t].wait()
            sends_in[n][t].wait_recv()
        for j in range(HEADS_PER_CHUNK):
            head(n * HEADS_PER_CHUNK + j)
        cols = pl.ds(n * CHUNK, CHUNK)
        group = []
        for slot in (2, 3, 1):
            group.append(
                remote(
                    vall.at[pl.ds(0, seq), cols],
                    vall.at[pl.ds(slot * seq, seq), cols],
                    v_send.at[n, slot - 1],
                    v_recv.at[n, slot - 1],
                    plane_id(slot // 2, slot % 2, 0)[0],
                )
            )
            group[-1].start()
        v_copies.append(group)
        out_cols = pl.ds(aligned(y * half + n * CHUNK), CHUNK)
        results = ((vall, dv_out), (dk_s, dk_out), (dq_s, dq_out))
        group = []
        for t, (src, dst) in enumerate(results):
            group.append(
                remote(
                    src.at[peer_rows, cols],
                    dst.at[:, out_cols],
                    r_send.at[n, t],
                    r_recv.at[n, t],
                    peer_id,
                )
            )
            group[-1].start()
        r_copies.append(group)
        group = []
        for t, (src, dst) in enumerate(results):
            group.append(
                pltpu.make_async_copy(
                    src.at[my_rows, cols], dst.at[:, out_cols], o_local.at[n, t]
                )
            )
            group[-1].start()
        o_copies.append(group)

    def weight(n):
        for copy in v_copies[n]:
            copy.wait_recv()
        cols = pl.ds(n * CHUNK, CHUNK)
        term = dot_plain(lt[...], vall[:, cols])
        w_own[:, cols] = term[:each]
        group = []
        for dz in range(1, nz):
            w_send[dz - 1, :, cols] = term[dz * each : (dz + 1) * each].astype(BF16)
            group.append(
                remote(
                    w_send.at[dz - 1, :, cols],
                    w_recv.at[dz - 1, :, cols],
                    z_send.at[n, dz - 1],
                    z_recv.at[n, dz - 1],
                    z_id(dz),
                )
            )
            group[-1].start()
        z_copies.append(group)

    attention(0)
    for n in range(1, chunks):
        attention(n)
        if n == 1:
            for copy in l_own:
                copy.wait()
            for copy in sends_l:
                copy.wait_recv()
            for s in range(4):
                lt[:, pl.ds(s * seq, seq)] = lall[pl.ds(s * seq, seq), :].T
        weight(n - 1)
    weight(chunks - 1)

    w_copies = []
    for n in range(chunks):
        cols = pl.ds(n * CHUNK, CHUNK)
        total = w_own[:, cols]
        for dz in range(1, nz):
            z_copies[n][dz - 1].wait_recv()
            total = total + w_recv[dz - 1, :, cols].astype(F32)
        w_own[:, cols] = total
        w_copies.append(
            pltpu.make_async_copy(w_own.at[:, cols], w_out.at[:, cols], w_local.at[n])
        )
        w_copies[-1].start()

    for copies in sends_in + v_copies + z_copies + [sends_l]:
        for copy in copies:
            copy.wait_send()
    for copies in r_copies + o_copies + [w_copies]:
        for copy in copies:
            copy.wait()


def store_kernel(a, b, c, d, a_out, b_out, c_out, d_out, sems):
    pairs = ((a, a_out), (b, b_out), (c, c_out), (d, d_out))
    copies = [pltpu.make_async_copy(i, o, sems.at[n]) for n, (i, o) in enumerate(pairs)]
    for copy in copies:
        copy.start()
    for copy in copies:
        copy.wait()


def fused_body(layer_input, queries, key_states, value_states, out_grad, block_kinds):
    rows, width = queries.shape[1:]
    half = width // 2
    nz = lax.axis_size("dp") // 4
    chunks = half // CHUNK
    seq = 2 * rows
    depth = 4 * seq
    each = HEAD_DIM
    dma = pltpu.SemaphoreType.DMA
    half_out = jax.ShapeDtypeStruct((rows, width), BF16)
    outs = pl.pallas_call(
        functools.partial(fused_kernel, (rows, half, nz, chunks)),
        out_shape=(half_out, half_out, half_out, jax.ShapeDtypeStruct((each, half), F32)),
        in_specs=[pl.BlockSpec(memory_space=pltpu.SMEM)]
        + [pl.BlockSpec(memory_space=pl.ANY)] * 5,
        out_specs=[pl.BlockSpec(memory_space=pl.ANY)] * 4,
        scratch_shapes=[
            pltpu.VMEM((4, seq, half), BF16),
            pltpu.VMEM((seq, half), BF16),
            pltpu.VMEM((seq, half), BF16),
            pltpu.VMEM((depth, half), BF16),
            pltpu.VMEM((depth, nz * each), BF16),
            pltpu.VMEM((nz * each, depth), BF16),
            pltpu.VMEM((nz - 1, each, half), BF16),
            pltpu.VMEM((nz - 1, each, half), BF16),
            pltpu.VMEM((each, half), F32),
            dma((chunks, 4)),
            dma((chunks, 4)),
            dma((chunks, 4)),
            dma((7, nz)),
            dma((7, nz)),
            dma((nz,)),
            dma((chunks, 3)),
            dma((chunks, 3)),
            dma((chunks, 3)),
            dma((chunks, 3)),
            dma((chunks, 3)),
            dma((chunks, nz - 1)),
            dma((chunks, nz - 1)),
            dma((chunks,)),
        ],
        compiler_params=pltpu.CompilerParams(
            collective_id=0, has_side_effects=True, vmem_limit_bytes=VMEM_LIMIT
        ),
        cost_estimate=pl.CostEstimate(
            flops=2 * (5 * seq * seq * half + depth * nz * each * half),
            bytes_accessed=8 * rows * width * 2 + each * half * 4,
            transcendentals=seq * seq * half // HEAD_DIM,
        ),
    )(block_kinds, layer_input[0], queries[0], key_states[0], value_states[0], out_grad[0])
    outs = pl.pallas_call(
        store_kernel,
        out_shape=tuple(jax.ShapeDtypeStruct(o.shape, o.dtype) for o in outs),
        in_specs=[pl.BlockSpec(memory_space=pltpu.VMEM)] * 4,
        out_specs=[pl.BlockSpec(memory_space=pl.ANY)] * 4,
        scratch_shapes=[dma((4,))],
        compiler_params=pltpu.CompilerParams(vmem_limit_bytes=VMEM_LIMIT),
        cost_estimate=pl.CostEstimate(flops=0, bytes_accessed=8 * rows * width * 2, transcendentals=0),
    )(*outs)
    return (outs[0][None], outs[1][None], outs[2][None], outs[3])


def pick_body(mesh):
    ctx_size, dp_size = mesh.shape["ctx"], mesh.shape["dp"]

    def chosen(layer_input, queries, *others):
        fits = (
            ctx_size == 2
            and dp_size % 4 == 0
            and dp_size > 4
            and dp_size * HEAD_DIM == D_IN
            and queries.shape[0] == 1
            and 2 * queries.shape[1] == FRAME
            and queries.shape[2] % (2 * CHUNK) == 0
        )
        return (fused_body if fits else body)(layer_input, queries, *others)

    return chosen


def solution(mesh):
    return jax.shard_map(
        pick_body(mesh),
        mesh=mesh,
        in_specs=(
            P("dp", "ctx", None),
            P("dp", "ctx", None),
            P("dp", "ctx", None),
            P("dp", "ctx", None),
            P("dp", "ctx", None),
            P("dp", None),
        ),
        out_specs=(
            P("dp", "ctx", None),
            P("dp", "ctx", None),
            P("dp", "ctx", None),
            P("dp", "ctx"),
        ),
        check_vma=False,
    )
```

```python
import functools

import jax
import jax.numpy as jnp
from jax import lax
from jax.experimental import pallas as pl
from jax.experimental.pallas import tpu as pltpu
from jax.sharding import PartitionSpec as P

FRAME = 256
HEAD_DIM = 128
D_IN = 2048


NEG_FILL = -1e30


def tile_scores(query_tile, key_block):
    product = jnp.einsum("ihd,jhd->hij", query_tile, key_block, preferred_element_type=jnp.float32)
    return product * HEAD_DIM ** (-0.5)


def tile_mask(row_start, key_start, key_count, block_kinds):
    query_pos = row_start + lax.iota(jnp.int32, FRAME)
    key_positions = key_start + lax.iota(jnp.int32, key_count)
    frame_flag = lax.dynamic_index_in_dim(block_kinds, row_start // FRAME, keepdims=False) == 1
    same_block = (key_positions // FRAME)[None, :] == (query_pos // FRAME)[:, None]
    return ((key_positions[None, :] <= query_pos[:, None]) | same_block & frame_flag)[None]


def rows_of(complete_rows, tile_index):
    return lax.dynamic_slice_in_dim(complete_rows, tile_index * FRAME, FRAME, 0)


def cols_of(stat_rows, tile_index):
    return lax.dynamic_slice_in_dim(stat_rows, tile_index * FRAME, FRAME, 1)


def put_cols(stat_rows, new_part, tile_index):
    return lax.dynamic_update_slice_in_dim(stat_rows, new_part, tile_index * FRAME, 1)


def head_split(stat_rows, work_items):
    pieces_out = []
    for work_item in work_items:
        pieces_out.append(stat_rows)
    return pieces_out


def sweep_peak(work_item, block_kinds):
    query_h, grad_h, key_block, value_block, key_start = work_item

    def advance(tile_index, peak_now):
        attention_scores = tile_scores(rows_of(query_h, tile_index), key_block)
        allowed = tile_mask(tile_index * FRAME, key_start, key_block.shape[0], block_kinds)
        return put_cols(
            peak_now, jnp.max(jnp.where(allowed, attention_scores, NEG_FILL), axis=2), tile_index
        )

    start_value = jnp.full((key_block.shape[1], query_h.shape[0]), NEG_FILL, jnp.float32)
    return lax.fori_loop(key_start // FRAME, query_h.shape[0] // FRAME, advance, start_value)


def sweep_total(work_item, block_kinds, peak_rows):
    query_h, grad_h, key_block, value_block, key_start = work_item

    def advance(tile_index, total_now):
        attention_scores = tile_scores(rows_of(query_h, tile_index), key_block)
        allowed = tile_mask(tile_index * FRAME, key_start, key_block.shape[0], block_kinds)
        shifted = jnp.exp(attention_scores - cols_of(peak_rows, tile_index)[:, :, None])
        return put_cols(total_now, jnp.sum(jnp.where(allowed, shifted, 0.0), axis=2), tile_index)

    start_value = jnp.zeros((key_block.shape[1], query_h.shape[0]), jnp.float32)
    return lax.fori_loop(key_start // FRAME, query_h.shape[0] // FRAME, advance, start_value)


def sweep_delta(work_item, block_kinds, log_rows):
    query_h, grad_h, key_block, value_block, key_start = work_item

    def advance(tile_index, delta_now):
        attention_scores = tile_scores(rows_of(query_h, tile_index), key_block)
        allowed = tile_mask(tile_index * FRAME, key_start, key_block.shape[0], block_kinds)
        weights = jnp.where(
            allowed, jnp.exp(attention_scores - cols_of(log_rows, tile_index)[:, :, None]), 0.0
        )
        grad_probs = jnp.einsum(
            "ihd,jhd->hij",
            rows_of(grad_h, tile_index),
            value_block,
            preferred_element_type=jnp.float32,
        )
        return put_cols(delta_now, jnp.sum(weights * grad_probs, axis=2), tile_index)

    start_value = jnp.zeros((key_block.shape[1], query_h.shape[0]), jnp.float32)
    return lax.fori_loop(key_start // FRAME, query_h.shape[0] // FRAME, advance, start_value)


def sweep_grads(work_item, block_kinds, log_rows, delta_rows):
    query_h, grad_h, key_block, value_block, key_start = work_item
    score_scale = HEAD_DIM ** (-0.5)

    def advance(tile_index, carry):
        key_acc, value_acc, dq_term = carry
        query_tile = rows_of(query_h, tile_index)
        gradient_piece = rows_of(grad_h, tile_index)
        attention_scores = tile_scores(query_tile, key_block)
        allowed = tile_mask(tile_index * FRAME, key_start, key_block.shape[0], block_kinds)
        weights = jnp.where(
            allowed, jnp.exp(attention_scores - cols_of(log_rows, tile_index)[:, :, None]), 0.0
        )
        grad_probs = jnp.einsum(
            "ihd,jhd->hij", gradient_piece, value_block, preferred_element_type=jnp.float32
        )
        grad_scores = (
            weights * (grad_probs - cols_of(delta_rows, tile_index)[:, :, None]) * score_scale
        ).astype(jnp.bfloat16)
        weights_half = weights.astype(jnp.bfloat16)
        value_acc = value_acc + jnp.einsum(
            "hij,ihd->jhd", weights_half, gradient_piece, preferred_element_type=jnp.float32
        )
        key_acc = key_acc + jnp.einsum(
            "hij,ihd->jhd", grad_scores, query_tile, preferred_element_type=jnp.float32
        )
        query_rows_part = jnp.einsum(
            "hij,jhd->ihd", grad_scores, key_block, preferred_element_type=jnp.float32
        )
        dq_term = lax.dynamic_update_slice_in_dim(dq_term, query_rows_part, tile_index * FRAME, 0)
        return (key_acc, value_acc, dq_term)

    start_value = (
        jnp.zeros(key_block.shape, jnp.float32),
        jnp.zeros(key_block.shape, jnp.float32),
        jnp.zeros(query_h.shape, jnp.float32),
    )
    return lax.fori_loop(key_start // FRAME, query_h.shape[0] // FRAME, advance, start_value)


def body(layer_input, queries, key_states, value_states, out_grad, block_kinds):
    shard_rows = queries.shape[1]
    row_width = queries.shape[2]
    head_count = row_width // HEAD_DIM
    ctx_size = lax.axis_size("ctx")
    dp_size = lax.axis_size("dp")
    my_index = lax.axis_index("ctx")
    kinds_row = block_kinds[0]
    query_all, grad_all = (
        lax.all_gather(queries[0], "ctx", axis=0, tiled=True),
        lax.all_gather(out_grad[0], "ctx", axis=0, tiled=True),
    )
    total_rows = query_all.shape[0]
    query_all = query_all.reshape(total_rows, head_count, HEAD_DIM)
    grad_all = grad_all.reshape(total_rows, head_count, HEAD_DIM)
    own_keys = key_states[0].reshape(shard_rows, head_count, HEAD_DIM)
    own_values = value_states[0].reshape(shard_rows, head_count, HEAD_DIM)
    own_start = my_index * shard_rows
    work_items = [(query_all, grad_all, own_keys, own_values, own_start)]
    row_peaks = jnp.concatenate(
        [sweep_peak(work_item, kinds_row) for work_item in work_items], axis=0
    )
    row_peaks = lax.pmax(row_peaks.astype(jnp.bfloat16), "ctx").astype(row_peaks.dtype)
    peak_parts = head_split(row_peaks, work_items)
    totals = jnp.concatenate(
        [
            sweep_total(work_item, kinds_row, peak_part)
            for work_item, peak_part in zip(work_items, peak_parts)
        ],
        axis=0,
    )
    totals = lax.psum(totals, "ctx")
    log_total = row_peaks + jnp.log(totals)
    log_parts = head_split(log_total, work_items)
    deltas = jnp.concatenate(
        [
            sweep_delta(work_item, kinds_row, log_part)
            for work_item, log_part in zip(work_items, log_parts)
        ],
        axis=0,
    )
    deltas = lax.psum(deltas, "ctx")
    delta_parts = head_split(deltas, work_items)
    results = [
        sweep_grads(work_item, kinds_row, log_part, delta_part)
        for work_item, log_part, delta_part in zip(work_items, log_parts, delta_parts)
    ]
    dq_term = jnp.concatenate([entry_set[2] for entry_set in results], axis=1).reshape(
        total_rows, row_width
    )
    query_grad = lax.psum_scatter(
        dq_term.astype(jnp.bfloat16), "ctx", scatter_dimension=0, tiled=True
    )
    key_grad = results[0][0].astype(jnp.bfloat16)
    value_grad = results[0][1].astype(jnp.bfloat16)
    key_grad = key_grad.reshape(shard_rows, row_width)
    value_grad = value_grad.reshape(shard_rows, row_width)
    rows_each = D_IN // dp_size
    cols_each = row_width // ctx_size
    divided_input = layer_input[0].reshape(shard_rows, dp_size, rows_each)
    divided_gradient = value_grad.reshape(shard_rows, ctx_size, cols_each)
    weight_term = jnp.einsum(
        "zkg,zbi->kbgi", divided_input, divided_gradient, preferred_element_type=jnp.float32
    )
    weight_term = weight_term.reshape(dp_size * ctx_size * rows_each, cols_each)
    weight_grad = lax.psum_scatter(weight_term, ("dp", "ctx"), scatter_dimension=0, tiled=True)
    return (query_grad[None], key_grad[None], value_grad[None], weight_grad)


HEADS_PER_CHUNK = 2
CHUNK = HEADS_PER_CHUNK * HEAD_DIM
VMEM_LIMIT = 63 * 1024 * 1024
MESH = pl.DeviceIdType.MESH
F32 = jnp.float32
BF16 = jnp.bfloat16
SCALE = HEAD_DIM ** (-0.5)
PLANE = [(dx, dc, dy) for dx in (0, 1) for dc in (0, 1) for dy in (0, 1)]


def dot_last(a, b):
    return lax.dot_general(a, b, (((1,), (1,)), ((), ())), preferred_element_type=F32)


def dot_first(a, b):
    return lax.dot_general(a, b, (((0,), (0,)), ((), ())), preferred_element_type=F32)


def dot_plain(a, b):
    return lax.dot_general(a, b, (((1,), (0,)), ((), ())), preferred_element_type=F32)


def fused_kernel(
    sizes,
    kinds,
    x_in,
    q_in,
    k_in,
    v_in,
    g_in,
    dq_out,
    dk_out,
    dv_out,
    w_out,
    qkvg,
    dq_s,
    dk_s,
    vall,
    lall,
    lt,
    w_send,
    w_recv,
    w_own,
    in_send,
    in_recv,
    in_local,
    l_send,
    l_recv,
    l_local,
    v_send,
    v_recv,
    r_send,
    r_recv,
    o_local,
    z_send,
    z_recv,
    w_local,
):
    rows, half, nz, chunks = sizes
    seq = 2 * rows
    each = HEAD_DIM
    dp = lax.axis_index("dp")
    y = lax.axis_index("ctx")
    c = lax.rem(dp, 2)
    x = lax.rem(dp // 2, 2)
    z = dp // 4
    yp = 1 - y

    def plane_id(dx, dc, dy):
        xx = lax.rem(x + dx, 2)
        cc = lax.rem(c + dc, 2)
        yy = lax.rem(y + dy, 2)
        return ((z * 2 + xx) * 2 + cc, yy), xx, cc

    def z_id(dz):
        return (lax.rem(z + dz, nz) * 4 + x * 2 + c, y)

    barrier = pltpu.get_barrier_semaphore()
    for dx, dc, dy in PLANE[1:]:
        pl.semaphore_signal(barrier, inc=1, device_id=plane_id(dx, dc, dy)[0], device_id_type=MESH)
    for dz in range(1, nz):
        pl.semaphore_signal(barrier, inc=1, device_id=z_id(dz), device_id_type=MESH)

    def aligned(value):
        return pl.multiple_of(value, 128)

    my_rows = pl.ds(aligned(y * rows), rows)
    peer_rows = pl.ds(aligned(yp * rows), rows)

    def remote(src, dst, send_sem, recv_sem, device):
        return pltpu.make_async_remote_copy(
            src_ref=src,
            dst_ref=dst,
            send_sem=send_sem,
            recv_sem=recv_sem,
            device_id=device,
            device_id_type=MESH,
        )

    sources = (q_in, k_in, v_in, g_in)
    local_in = []
    for n in range(chunks):
        cols = pl.ds(n * CHUNK, CHUNK)
        mine = pl.ds(aligned(y * half + n * CHUNK), CHUNK)
        local_in.append(
            [
                pltpu.make_async_copy(
                    src.at[:, mine], qkvg.at[t, my_rows, cols], in_local.at[n, t]
                )
                for t, src in enumerate(sources)
            ]
        )
    for copies in local_in:
        for copy in copies:
            copy.start()
    l_own = []
    for dz in range(nz):
        col = pl.ds(aligned((lax.rem(z + dz, nz) * 4 + x * 2 + c) * each), each)
        l_own.append(
            pltpu.make_async_copy(
                x_in.at[:, col], lall.at[my_rows, pl.ds(dz * each, each)], l_local.at[dz]
            )
        )
        l_own[-1].start()

    pl.semaphore_wait(barrier, 7 + nz - 1)

    peer_id = plane_id(0, 0, 1)[0]
    sends_in = []
    for n in range(chunks):
        cols = pl.ds(n * CHUNK, CHUNK)
        theirs = pl.ds(aligned(yp * half + n * CHUNK), CHUNK)
        sends_in.append(
            [
                remote(
                    src.at[:, theirs],
                    qkvg.at[t, my_rows, cols],
                    in_send.at[n, t],
                    in_recv.at[n, t],
                    peer_id,
                )
                for t, src in enumerate(sources)
            ]
        )
    sends_l = []
    for p, (dx, dc, dy) in enumerate(PLANE):
        if p == 0:
            continue
        device, xx, cc = plane_id(dx, dc, dy)
        slot = dx * 2 + dc
        dst_rows = pl.ds(aligned(slot * seq + y * rows), rows)
        for dz in range(nz):
            col = pl.ds(aligned((lax.rem(z + dz, nz) * 4 + xx * 2 + cc) * each), each)
            sends_l.append(
                remote(
                    x_in.at[:, col],
                    lall.at[dst_rows, pl.ds(dz * each, each)],
                    l_send.at[p - 1, dz],
                    l_recv.at[p - 1, dz],
                    device,
                )
            )
    for n in range(chunks):
        for copy in sends_in[n]:
            copy.start()
        if n == 0:
            for copy in sends_l:
                copy.start()

    key_pos = lax.broadcasted_iota(jnp.int32, (seq, seq), 0)
    query_pos = lax.broadcasted_iota(jnp.int32, (seq, seq), 1)
    allowed = key_pos <= query_pos + kinds[0, 0] * seq

    def head(h):
        hc = pl.ds(h * HEAD_DIM, HEAD_DIM)
        q = qkvg[0, :, hc]
        k = qkvg[1, :, hc]
        v = qkvg[2, :, hc]
        g = qkvg[3, :, hc]
        scores = jnp.where(allowed, dot_last(k, q) * SCALE, NEG_FILL)
        peak = jnp.max(scores, axis=0, keepdims=True)
        p = jnp.exp(scores - peak)
        weights = p * (1.0 / jnp.sum(p, axis=0, keepdims=True))
        weights_half = weights.astype(BF16)
        vall[pl.ds(0, seq), hc] = dot_plain(weights_half, g).astype(BF16)
        grad_probs = dot_last(v, g)
        delta = jnp.sum(weights * grad_probs, axis=0, keepdims=True)
        grad_scores = (weights * (grad_probs - delta) * SCALE).astype(BF16)
        dk_s[:, hc] = dot_plain(grad_scores, q).astype(BF16)
        parts = [
            dot_first(grad_scores[s * rows : (s + 1) * rows], k[s * rows : (s + 1) * rows])
            .astype(BF16)
            .astype(F32)
            for s in range(2)
        ]
        dq_s[:, hc] = (parts[0] + parts[1]).astype(BF16)

    v_copies, r_copies, z_copies, o_copies = [], [], [], []

    def attention(n):
        for t in range(4):
            local_in[n][t].wait()
            sends_in[n][t].wait_recv()
        for j in range(HEADS_PER_CHUNK):
            head(n * HEADS_PER_CHUNK + j)
        cols = pl.ds(n * CHUNK, CHUNK)
        group = []
        for slot in (2, 3, 1):
            group.append(
                remote(
                    vall.at[pl.ds(0, seq), cols],
                    vall.at[pl.ds(slot * seq, seq), cols],
                    v_send.at[n, slot - 1],
                    v_recv.at[n, slot - 1],
                    plane_id(slot // 2, slot % 2, 0)[0],
                )
            )
            group[-1].start()
        v_copies.append(group)
        out_cols = pl.ds(aligned(y * half + n * CHUNK), CHUNK)
        results = ((vall, dv_out), (dk_s, dk_out), (dq_s, dq_out))
        group = []
        for t, (src, dst) in enumerate(results):
            group.append(
                remote(
                    src.at[peer_rows, cols],
                    dst.at[:, out_cols],
                    r_send.at[n, t],
                    r_recv.at[n, t],
                    peer_id,
                )
            )
            group[-1].start()
        r_copies.append(group)
        group = []
        for t, (src, dst) in enumerate(results):
            group.append(
                pltpu.make_async_copy(
                    src.at[my_rows, cols], dst.at[:, out_cols], o_local.at[n, t]
                )
            )
            group[-1].start()
        o_copies.append(group)

    def weight(n):
        for copy in v_copies[n]:
            copy.wait_recv()
        cols = pl.ds(n * CHUNK, CHUNK)
        term = dot_plain(lt[...], vall[:, cols])
        w_own[:, cols] = term[:each]
        group = []
        for dz in range(1, nz):
            w_send[dz - 1, :, cols] = term[dz * each : (dz + 1) * each].astype(BF16)
            group.append(
                remote(
                    w_send.at[dz - 1, :, cols],
                    w_recv.at[dz - 1, :, cols],
                    z_send.at[n, dz - 1],
                    z_recv.at[n, dz - 1],
                    z_id(dz),
                )
            )
            group[-1].start()
        z_copies.append(group)

    attention(0)
    for n in range(1, chunks):
        attention(n)
        if n == 1:
            for copy in l_own:
                copy.wait()
            for copy in sends_l:
                copy.wait_recv()
            for s in range(4):
                lt[:, pl.ds(s * seq, seq)] = lall[pl.ds(s * seq, seq), :].T
        weight(n - 1)
    weight(chunks - 1)

    w_copies = []
    for n in range(chunks):
        cols = pl.ds(n * CHUNK, CHUNK)
        total = w_own[:, cols]
        for dz in range(1, nz):
            z_copies[n][dz - 1].wait_recv()
            total = total + w_recv[dz - 1, :, cols].astype(F32)
        w_own[:, cols] = total
        w_copies.append(
            pltpu.make_async_copy(w_own.at[:, cols], w_out.at[:, cols], w_local.at[n])
        )
        w_copies[-1].start()

    for copies in sends_in + v_copies + z_copies + [sends_l]:
        for copy in copies:
            copy.wait_send()
    for copies in r_copies + o_copies + [w_copies]:
        for copy in copies:
            copy.wait()


def store_kernel(a, b, c, d, a_out, b_out, c_out, d_out, a_s, b_s, c_s, d_s, load, store):
    stages = ((a, a_s, a_out), (b, b_s, b_out), (c, c_s, c_out), (d, d_s, d_out))
    loads, stores = [], []
    for n, (src, mid, dst) in enumerate(stages):
        part = src.shape[0] // 2
        for p in range(2):
            piece = pl.ds(p * part, part)
            loads.append(pltpu.make_async_copy(src.at[piece], mid.at[piece], load.at[n, p]))
            stores.append(pltpu.make_async_copy(mid.at[piece], dst.at[piece], store.at[n, p]))
    for copy in loads:
        copy.start()
    for copy_in, copy_out in zip(loads, stores):
        copy_in.wait()
        copy_out.start()
    for copy in stores:
        copy.wait()


def fused_body(layer_input, queries, key_states, value_states, out_grad, block_kinds):
    rows, width = queries.shape[1:]
    half = width // 2
    nz = lax.axis_size("dp") // 4
    chunks = half // CHUNK
    seq = 2 * rows
    depth = 4 * seq
    each = HEAD_DIM
    dma = pltpu.SemaphoreType.DMA
    half_out = jax.ShapeDtypeStruct((rows, width), BF16)
    outs = pl.pallas_call(
        functools.partial(fused_kernel, (rows, half, nz, chunks)),
        out_shape=(half_out, half_out, half_out, jax.ShapeDtypeStruct((each, half), F32)),
        in_specs=[pl.BlockSpec(memory_space=pltpu.SMEM)]
        + [pl.BlockSpec(memory_space=pl.ANY)] * 5,
        out_specs=[pl.BlockSpec(memory_space=pl.ANY)] * 4,
        scratch_shapes=[
            pltpu.VMEM((4, seq, half), BF16),
            pltpu.VMEM((seq, half), BF16),
            pltpu.VMEM((seq, half), BF16),
            pltpu.VMEM((depth, half), BF16),
            pltpu.VMEM((depth, nz * each), BF16),
            pltpu.VMEM((nz * each, depth), BF16),
            pltpu.VMEM((nz - 1, each, half), BF16),
            pltpu.VMEM((nz - 1, each, half), BF16),
            pltpu.VMEM((each, half), F32),
            dma((chunks, 4)),
            dma((chunks, 4)),
            dma((chunks, 4)),
            dma((7, nz)),
            dma((7, nz)),
            dma((nz,)),
            dma((chunks, 3)),
            dma((chunks, 3)),
            dma((chunks, 3)),
            dma((chunks, 3)),
            dma((chunks, 3)),
            dma((chunks, nz - 1)),
            dma((chunks, nz - 1)),
            dma((chunks,)),
        ],
        compiler_params=pltpu.CompilerParams(
            collective_id=0, has_side_effects=True, vmem_limit_bytes=VMEM_LIMIT
        ),
        cost_estimate=pl.CostEstimate(
            flops=2 * (5 * seq * seq * half + depth * nz * each * half),
            bytes_accessed=8 * rows * width * 2 + each * half * 4,
            transcendentals=seq * seq * half // HEAD_DIM,
        ),
    )(block_kinds, layer_input[0], queries[0], key_states[0], value_states[0], out_grad[0])
    outs = pl.pallas_call(
        store_kernel,
        out_shape=tuple(jax.ShapeDtypeStruct(o.shape, o.dtype) for o in outs),
        in_specs=[pl.BlockSpec(memory_space=pl.ANY)] * 4,
        out_specs=[pl.BlockSpec(memory_space=pl.ANY)] * 4,
        scratch_shapes=[pltpu.VMEM(o.shape, o.dtype) for o in outs] + [dma((4, 2))] * 2,
        compiler_params=pltpu.CompilerParams(vmem_limit_bytes=VMEM_LIMIT),
        cost_estimate=pl.CostEstimate(flops=0, bytes_accessed=8 * rows * width * 2, transcendentals=0),
    )(*outs)
    return (outs[0][None], outs[1][None], outs[2][None], outs[3])


def pick_body(mesh):
    ctx_size, dp_size = mesh.shape["ctx"], mesh.shape["dp"]

    def chosen(layer_input, queries, *others):
        fits = (
            ctx_size == 2
            and dp_size % 4 == 0
            and dp_size > 4
            and dp_size * HEAD_DIM == D_IN
            and queries.shape[0] == 1
            and 2 * queries.shape[1] == FRAME
            and queries.shape[2] % (2 * CHUNK) == 0
        )
        return (fused_body if fits else body)(layer_input, queries, *others)

    return chosen


def solution(mesh):
    return jax.shard_map(
        pick_body(mesh),
        mesh=mesh,
        in_specs=(
            P("dp", "ctx", None),
            P("dp", "ctx", None),
            P("dp", "ctx", None),
            P("dp", "ctx", None),
            P("dp", "ctx", None),
            P("dp", None),
        ),
        out_specs=(
            P("dp", "ctx", None),
            P("dp", "ctx", None),
            P("dp", "ctx", None),
            P("dp", "ctx"),
        ),
        check_vma=False,
    )
```
